32 devices in a mesh: aa: 4 (over z), ba: 8 (over y, x, core).
Axes of the slice: x: 2, y: 2, z: 4, core: 2. Of those that a mesh axis runs over, the one named last changes fastest.
Arguments:
- corr_old: bfloat16 [14336, 28672], P('aa', 'ba'), may hold values from -0.19921875 to 0.19921875
- store_a: bfloat16 [2048, 14336], P('ba', 'aa'), may hold values from -6 to 6
- store_b: bfloat16 [2048, 28672], P('aa', 'ba'), may hold values from -6 to 6
- shuffle_order: int32 [2048], replicated, may hold values from 0 to 2047, each once
Outputs:
- current_comovement: bfloat16 [14336, 28672], P('aa', 'ba')
- source_multiplier: float32 [14336], P('aa')
- column_multiplier: float32 [28672], P('ba')
The draws below stay inside these ranges and needn't reach their ends.
Inputs may be any that keep to these rules, and one draw needn't show every extreme that they name: `shuffle_order`: a permutation of the store's rows.
All inputs are finite; a program needn't handle non-finite values.
Results may differ from the reference program's by a relative error of at most 0.0068.
Values may be sent and summed in bfloat16 or wider, within the bound.
A program may use at most 192 MiB of HBM per device.

```python
import jax
import jax.numpy as jnp
from jax import lax

LEFT_NEURONS = 14336
RIGHT_NEURONS = 28672
GROUP = 1024
ITERS = 3
STORE = 2048
N_AA = 4


def levels(stream_key, extent, shards, smallest, high):
    def one(dim, shards_of):
        draws = jax.random.uniform(jax.random.fold_in(jax.random.fold_in(stream_key, 6), dim), (shards_of,), jnp.float32, smallest / len(shards), high / len(shards))
        return jnp.repeat(jnp.exp(draws), extent[dim] // shards_of).reshape((-1,) + (1,) * (len(extent) - dim - 1))

    loudness = one(*shards[0])
    for cut in shards[1:]:
        loudness = loudness * one(*cut)
    return loudness


def normal_values(key, dims, spread, most, pieces=(), kind=jnp.bfloat16):
    level = levels(key, dims, pieces, -0.22, 0.18) if pieces else 1.0
    drawn = jax.random.normal(key, dims, jnp.float32) * spread * level
    return jnp.minimum(jnp.maximum(drawn, -most), most).astype(kind)


def setup_inputs(seed: int = 0) -> dict:
    key_of = jax.random.split(jax.random.key(seed), 5)
    corr_old = normal_values(key_of[0], (LEFT_NEURONS, RIGHT_NEURONS), 0.03, 0.19921875, ((0, 4), (1, 8)))
    store_a = normal_values(key_of[1], (STORE, LEFT_NEURONS), 1.0, 6.0, ((0, 8), (1, 4)))
    store_b = normal_values(key_of[2], (STORE, RIGHT_NEURONS), 1.0, 6.0, ((0, 4), (1, 8)))
    shuffle_order = jax.random.permutation(key_of[3], STORE).astype(jnp.int32)
    return {"corr_old": corr_old, "store_a": store_a, "store_b": store_b, "shuffle_order": shuffle_order}


decay_factor = 0.5
regularizer_strength = 0.01


def reference(corr_old, store_a, store_b, shuffle_order):
    selected_entries = shuffle_order[:GROUP]
    sel_a = jnp.take(store_a, selected_entries, axis=0).astype(jnp.float32)
    sel_b = jnp.take(store_b, selected_entries, axis=0).astype(jnp.float32)
    submatrix_piece = LEFT_NEURONS // N_AA
    first_model_blocks = sel_a.reshape(GROUP, N_AA, submatrix_piece).transpose(1, 0, 2)
    old_blocks = corr_old.reshape(N_AA, submatrix_piece, RIGHT_NEURONS)

    def one_block(pair):
        a_part, old_part = pair
        summed = jnp.einsum("ti,tj->ij", a_part, sel_b)
        return (decay_factor * old_part.astype(jnp.float32) + (1.0 - decay_factor) / GROUP * summed).astype(jnp.bfloat16)

    incoming_submatrices = lax.map(one_block, (first_model_blocks, old_blocks))
    current_comovement = incoming_submatrices.reshape(LEFT_NEURONS, RIGHT_NEURONS)

    def make_kernel(submatrix_extract):
        return jnp.exp(submatrix_extract.astype(jnp.float32) / regularizer_strength).astype(jnp.bfloat16)

    kernel_blocks = lax.map(make_kernel, incoming_submatrices)
    column_multiplier = jnp.ones((RIGHT_NEURONS,), jnp.float32)
    source_multiplier = jnp.ones((LEFT_NEURONS,), jnp.float32)
    for step in range(ITERS):
        scale_b = column_multiplier.astype(jnp.bfloat16)

        def row_part(kernel_tile, scale_b=scale_b):
            return jnp.dot(kernel_tile, scale_b, preferred_element_type=jnp.float32)

        source_marginal = lax.map(row_part, kernel_blocks).reshape(LEFT_NEURONS)
        source_multiplier = RIGHT_NEURONS / source_marginal

        def append_columns(acc, pair):
            kernel_tile, scale_a = pair
            return acc + jnp.dot(scale_a, kernel_tile, preferred_element_type=jnp.float32), None

        scale_rows = source_multiplier.astype(jnp.bfloat16).reshape(N_AA, submatrix_piece)
        column_marginal = lax.scan(append_columns, jnp.zeros((RIGHT_NEURONS,), jnp.float32), (kernel_blocks, scale_rows))[0]
        column_multiplier = LEFT_NEURONS / column_marginal
    return current_comovement, source_multiplier, column_multiplier
```

```python
import functools

import jax
import jax.numpy as jnp
from jax import lax
from jax.experimental import pallas as pl
from jax.experimental.pallas import tpu as pltpu
from jax.sharding import PartitionSpec as P

GROUP = 1024
ITERS = 3
MESH = pl.DeviceIdType.MESH

decay_factor = 0.5
regularizer_strength = 0.01

CHUNK = 256
AHEAD = 3
FIRST = 4


def contract(left, right):
    return lax.dot_general(
        left, right, (((0,), (0,)), ((), ())), preferred_element_type=jnp.float32
    )


def kernel(na, nb, S, W, bp, ap, corr, com, src_out, col_out,
           K, AT, B, cbuf, obuf, apart, aown, rs, rowx, colx,
           b_send, b_recv, b_loc, a_send, a_recv, f_send, p_sem, a_loc,
           c_sem, o_sem, r_send, r_recv, k_send, k_recv):
    ia, ib = lax.axis_index("aa"), lax.axis_index("ba")
    Q = W // CHUNK
    H = W // 2
    R = 512 if W % 512 == 0 else 256
    c = lax.rem(ib, 2)
    sa = ib // 2
    sib = ib + 1 - 2 * c

    barrier = pltpu.get_barrier_semaphore()
    for d in range(1, na):
        pl.semaphore_signal(barrier, inc=1, device_id=(lax.rem(ia + d, na), ib), device_id_type=MESH)
    for d in range(1, nb):
        pl.semaphore_signal(barrier, inc=1, device_id=(ia, lax.rem(ib + d, nb)), device_id_type=MESH)

    def corr_copy(q):
        slot = lax.rem(q, 2)
        return pltpu.make_async_copy(
            corr.at[:, pl.ds(pl.multiple_of(q * CHUNK, CHUNK), CHUNK)], cbuf.at[slot], c_sem.at[slot])

    def out_copy(q):
        slot = lax.rem(q, 2)
        return pltpu.make_async_copy(
            obuf.at[slot], com.at[:, pl.ds(pl.multiple_of(q * CHUNK, CHUNK), CHUNK)], o_sem.at[slot])

    def half(ref, h):
        return ref.at[:, pl.ds(pl.multiple_of(h * H, 128), H)]

    own_a = pltpu.make_async_copy(half(ap, c), aown, a_loc)
    own_a.start()
    corr_copy(0).start()
    rs[...] = jnp.zeros_like(rs)
    pl.semaphore_wait(barrier, na + nb - 2)

    part = pltpu.make_async_remote_copy(
        src_ref=half(ap, 1 - c), dst_ref=apart, send_sem=p_sem.at[0], recv_sem=p_sem.at[1],
        device_id=(ia, sib), device_id_type=MESH)
    part.start()

    def b_slot(s, t):
        return B.at[t, pl.ds(pl.multiple_of(s * S, 16), S)]

    def b_src(t):
        return bp.at[:, pl.ds(pl.multiple_of(t * CHUNK, CHUNK), CHUNK)]

    def b_copy(up, s, t, source):
        return pltpu.make_async_remote_copy(
            src_ref=source, dst_ref=b_slot(s, t), send_sem=b_send.at[up, s, t], recv_sem=b_recv.at[s, t],
            device_id=(ia + 1 if up == 0 else ia - 1, ib), device_id_type=MESH)

    def b_own(t):
        @pl.when(ia < na - 1)
        def _():
            b_copy(0, ia, t, b_src(t)).start()

        @pl.when(ia > 0)
        def _():
            b_copy(1, ia, t, b_src(t)).start()

        pltpu.make_async_copy(b_src(t), b_slot(ia, t), b_loc.at[t]).start()

    def comm(t):
        @pl.when(t + AHEAD < Q)
        def _():
            b_own(t + AHEAD)

        for d in range(1, na):
            @pl.when(ia - d >= 0)
            def _():
                s = ia - d
                b_copy(0, s, t, b_slot(s, t)).wait_recv()

                @pl.when(ia < na - 1)
                def _():
                    b_copy(0, s, t, b_slot(s, t)).start()

            @pl.when(ia + d < na)
            def _():
                s = ia + d
                b_copy(1, s, t, b_slot(s, t)).wait_recv()

                @pl.when(ia > 0)
                def _():
                    b_copy(1, s, t, b_slot(s, t)).start()

        pltpu.make_async_copy(b_src(t), b_slot(ia, t), b_loc.at[t]).wait()

    def a_slot(p, h):
        return K.at[pl.ds(pl.multiple_of(p * S, 16), S), pl.ds(pl.multiple_of(h * H, 128), H)]

    def a_copy(p, d):
        return pltpu.make_async_remote_copy(
            src_ref=a_slot(p, c), dst_ref=a_slot(p, c), send_sem=a_send.at[d], recv_sem=a_recv.at[p, c],
            device_id=(ia, lax.rem(ib + 2 * d, nb)), device_id_type=MESH)

    def a_forward(p, h):
        return pltpu.make_async_remote_copy(
            src_ref=a_slot(p, h), dst_ref=a_slot(p, h), send_sem=f_send.at[p], recv_sem=a_recv.at[p, h],
            device_id=(ia, sib), device_id_type=MESH)

    for t in range(min(AHEAD, Q)):
        b_own(t)
    own_a.wait()
    part.wait()
    a_slot(sa, c)[...] = aown[...] + apart[...]
    for d in range(1, na):
        a_copy(sa, d).start()
    a_forward(sa, c).start()

    def early(t, carry):
        comm(t)
        return carry

    lax.fori_loop(0, FIRST, early, 0)
    for d in range(1, na):
        p = lax.rem(sa + na - d, na)
        a_copy(p, d).wait_recv()
        a_forward(p, c).start()
    for p in range(na):
        a_forward(p, 1 - c).wait_recv()

    def turn(i, carry):
        cols = pl.ds(pl.multiple_of(i * 256, 256), 256)
        AT[cols, :] = K[0:na * S, cols].T
        return carry

    lax.fori_loop(0, W // 256, turn, 0)
    for d in range(1, na):
        a_copy(sa, d).wait_send()
    for p in range(na):
        a_forward(p, c).wait_send()

    ones = jnp.ones((16, CHUNK), jnp.bfloat16)

    def compute(q, carry):
        slot = lax.rem(q, 2)
        corr_copy(q).wait()

        @pl.when(q + 1 < Q)
        def _():
            corr_copy(q + 1).start()

        @pl.when(q >= 2)
        def _():
            out_copy(q - 2).wait()

        cols = pl.ds(pl.multiple_of(q * CHUNK, CHUNK), CHUNK)

        def block(r, carry):
            rows = pl.ds(pl.multiple_of(r * R, R), R)
            acc = jnp.dot(AT[rows, :], B[q], preferred_element_type=jnp.float32)
            cm = (decay_factor * cbuf[slot, rows, :].astype(jnp.float32)
                  + (1.0 - decay_factor) / GROUP * acc).astype(jnp.bfloat16)
            obuf[slot, rows, :] = cm
            e = jnp.exp(cm.astype(jnp.float32) * (1.0 / regularizer_strength)).astype(jnp.bfloat16)
            K[rows, cols] = e
            rs[:, rows] += lax.dot_general(
                ones, e, (((1,), (1,)), ((), ())), preferred_element_type=jnp.float32)
            return carry

        lax.fori_loop(0, W // R, block, 0)
        out_copy(q).start()
        return carry

    def done(t):
        return jnp.maximum(jnp.minimum(2 * (t - FIRST + 1), t), 0)

    def main(t, carry):
        comm(t)
        lax.fori_loop(done(t - 1), done(t), compute, 0)
        return carry

    lax.fori_loop(FIRST, Q, main, 0)
    lax.fori_loop(min(2 * (Q - FIRST), Q - 1), Q, compute, 0)

    def exchange(it, n, me, peer, buf, send, recv, partial):
        buf[it * n + me] = partial

        def copy(owner, d):
            return pltpu.make_async_remote_copy(
                src_ref=buf.at[it * n + owner], dst_ref=buf.at[it * n + owner],
                send_sem=send.at[it, d], recv_sem=recv.at[it, owner],
                device_id=peer(lax.rem(me + d, n)), device_id_type=MESH)

        for d in range(1, n):
            copy(me, d).start()
        for d in range(1, n):
            copy(lax.rem(me + n - d, n), d).wait_recv()
        total = buf[it * n]
        for j in range(1, n):
            total = total + buf[it * n + j]
        for d in range(1, n):
            copy(me, d).wait_send()
        return total

    def row_pass(colm):
        lhs = jnp.broadcast_to(colm, (16, W)).astype(jnp.bfloat16)

        def body(r, carry):
            rows = pl.ds(pl.multiple_of(r * R, R), R)
            rs[:, rows] = lax.dot_general(
                lhs, K[rows, :], (((1,), (1,)), ((), ())), preferred_element_type=jnp.float32)
            return carry

        lax.fori_loop(0, W // R, body, 0)
        return rs[0:1, :]

    def col_pass(srcm):
        lhs = jnp.broadcast_to(srcm, (16, W)).astype(jnp.bfloat16)

        def body(r, carry):
            cols = pl.ds(pl.multiple_of(r * R, R), R)
            rs[:, cols] = jnp.dot(lhs, K[:, cols], preferred_element_type=jnp.float32)
            return carry

        lax.fori_loop(0, W // R, body, 0)
        return rs[0:1, :]

    partial = rs[0:1, :]
    for it in range(ITERS):
        if it > 0:
            partial = row_pass(col_out[...])
        row = exchange(it, nb, ib, lambda j: (ia, j), rowx, r_send, r_recv, partial)
        src_out[...] = (nb * W) / row
        partial = col_pass(src_out[...])
        col = exchange(it, na, ia, lambda j: (j, ib), colx, k_send, k_recv, partial)
        col_out[...] = (na * W) / col

    for q in range(max(Q - 2, 0), Q):
        out_copy(q).wait()

    def drain(t, carry):
        for s in range(na):
            @pl.when((ia < na - 1) & (s <= ia))
            def _():
                b_copy(0, s, t, b_slot(s, t)).wait_send()

            @pl.when((ia > 0) & (s >= ia))
            def _():
                b_copy(1, s, t, b_slot(s, t)).wait_send()
        return carry

    lax.fori_loop(0, Q, drain, 0)


def fused(na, nb, S, W, bp, ap, corr):
    Q = W // CHUNK
    dma = pltpu.SemaphoreType.DMA
    any_space = pl.BlockSpec(memory_space=pl.ANY)
    vmem = pl.BlockSpec(memory_space=pltpu.VMEM)
    return pl.pallas_call(
        functools.partial(kernel, na, nb, S, W),
        out_shape=(
            jax.ShapeDtypeStruct((W, W), jnp.bfloat16),
            jax.ShapeDtypeStruct((1, W), jnp.float32),
            jax.ShapeDtypeStruct((1, W), jnp.float32),
        ),
        in_specs=[any_space] * 3,
        out_specs=(any_space, vmem, vmem),
        scratch_shapes=[
            pltpu.VMEM((W, W), jnp.bfloat16),
            pltpu.VMEM((W, na * S), jnp.bfloat16),
            pltpu.VMEM((Q, na * S, CHUNK), jnp.bfloat16),
            pltpu.VMEM((2, W, CHUNK), jnp.bfloat16),
            pltpu.VMEM((2, W, CHUNK), jnp.bfloat16),
            pltpu.VMEM((S, W // 2), jnp.bfloat16),
            pltpu.VMEM((S, W // 2), jnp.bfloat16),
            pltpu.VMEM((16, W), jnp.float32),
            pltpu.VMEM((ITERS * nb, 1, W), jnp.float32),
            pltpu.VMEM((ITERS * na, 1, W), jnp.float32),
            dma((2, na, Q)), dma((na, Q)), dma((Q,)),
            dma((na,)), dma((na, 2)), dma((na,)), dma((2,)), dma,
            dma((2,)), dma((2,)),
            dma((ITERS, nb)), dma((ITERS, nb)), dma((ITERS, na)), dma((ITERS, na)),
        ],
        compiler_params=pltpu.CompilerParams(
            collective_id=0, has_side_effects=True, vmem_limit_bytes=60 * 2**20),
        cost_estimate=pl.CostEstimate(
            flops=2 * GROUP * W * W, bytes_accessed=4 * W * W, transcendentals=W * W),
    )(bp, ap, corr)


def general(na, nb, corr_old, store_a, store_b, shuffle_order):
    rows_local = store_a.shape[0]
    chosen = jnp.zeros((shuffle_order.shape[0],), jnp.float32).at[shuffle_order[:GROUP]].set(1.0)
    kept_rows = lax.dynamic_slice_in_dim(chosen, lax.axis_index("ba") * rows_local, rows_local, 0)
    masked_a = store_a * kept_rows[:, None].astype(jnp.bfloat16)
    whole_a = lax.all_gather(masked_a, "ba", axis=0, tiled=True)
    summed = contract(whole_a, lax.all_gather(store_b, "aa", axis=0, tiled=True))
    com = (
        decay_factor * corr_old.astype(jnp.float32) + (1.0 - decay_factor) / GROUP * summed
    ).astype(jnp.bfloat16)
    K = jnp.exp(com.astype(jnp.float32) / regularizer_strength).astype(jnp.bfloat16)
    W = store_b.shape[1]
    col = jnp.ones((W,), jnp.float32)
    src = jnp.ones((store_a.shape[1],), jnp.float32)
    for _ in range(ITERS):
        src = nb * W / lax.psum(
            jnp.dot(K, col.astype(jnp.bfloat16), preferred_element_type=jnp.float32), "ba")
        col = na * store_a.shape[1] / lax.psum(
            jnp.dot(src.astype(jnp.bfloat16), K, preferred_element_type=jnp.float32), "aa")
    return com, src[None], col[None]


def shards(na, nb, corr_old, store_a, store_b, shuffle_order):
    ia, ib = lax.axis_index("aa"), lax.axis_index("ba")
    L, La = store_b.shape[0], store_a.shape[0]
    W = store_b.shape[1]
    step = max(16, 128 // na)
    S = -(-(GROUP // na + 32) // step) * step
    group = shuffle_order[:GROUP]
    owner = group // L
    order = jnp.arange(GROUP)

    def slots(seg):
        mine = owner == seg
        rank = jnp.sum((mine[None, :] & (order[None, :] < order[:, None])).astype(jnp.int32), axis=1)
        hit = mine[None, :] & (rank[None, :] == jnp.arange(S)[:, None])
        return jnp.sum(jnp.where(hit, group[None, :] + 1, 0), axis=1) - 1

    def pick(rows, first, store):
        hot = (rows[:, None] == first + jnp.arange(store.shape[0])[None, :]).astype(jnp.bfloat16)
        return jnp.dot(hot, store, preferred_element_type=jnp.float32).astype(jnp.bfloat16)

    fits = jnp.max(jnp.sum((owner[:, None] == jnp.arange(na)[None, :]).astype(jnp.int32), axis=0)) <= S

    def fast(corr_old, store_a, store_b, shuffle_order):
        bp = pick(slots(ia), ia * L, store_b)
        ap = pick(slots(ib // 2), ib * La, store_a)
        return fused(na, nb, S, W, bp, ap, corr_old)

    com, src, col = lax.cond(
        fits, fast, functools.partial(general, na, nb), corr_old, store_a, store_b, shuffle_order)
    return com, src[0], col[0]


def solution(mesh):
    na, nb = mesh.shape["aa"], mesh.shape["ba"]
    in_specs = (P("aa", "ba"), P("ba", "aa"), P("aa", "ba"), P())
    out_specs = (P("aa", "ba"), P("aa"), P("ba"))
    return jax.shard_map(
        functools.partial(shards, na, nb), mesh=mesh, in_specs=in_specs, out_specs=out_specs, check_vma=False)
```

```python
import functools

import jax
import jax.numpy as jnp
from jax import lax
from jax.experimental import pallas as pl
from jax.experimental.pallas import tpu as pltpu
from jax.sharding import PartitionSpec as P

GROUP = 1024
ITERS = 3
MESH = pl.DeviceIdType.MESH

decay_factor = 0.5
regularizer_strength = 0.01

CHUNK = 256
FIRST = 2


def contract(left, right):
    return lax.dot_general(
        left, right, (((0,), (0,)), ((), ())), preferred_element_type=jnp.float32
    )


def kernel(na, nb, S, W, hot_b, hot_a, store_b, store_a, corr, com, src_out, col_out,
           K, AT, B, cbuf, obuf, apart, asend, rs, rowx, colx,
           b_send, b_recv, a_send, a_recv, f_send, p_sem, l_sem,
           c_sem, o_sem, r_send, r_recv, k_send, k_recv):
    ia, ib = lax.axis_index("aa"), lax.axis_index("ba")
    Q = W // CHUNK
    H = W // 2
    R = 512 if W % 512 == 0 else 256
    c = lax.rem(ib, 2)
    sa = ib // 2
    sib = ib + 1 - 2 * c

    barrier = pltpu.get_barrier_semaphore()
    for d in range(1, na):
        pl.semaphore_signal(barrier, inc=1, device_id=(lax.rem(ia + d, na), ib), device_id_type=MESH)
    for d in range(1, nb):
        pl.semaphore_signal(barrier, inc=1, device_id=(ia, lax.rem(ib + d, nb)), device_id_type=MESH)

    def corr_copy(q):
        slot = lax.rem(q, 2)
        return pltpu.make_async_copy(
            corr.at[:, pl.ds(pl.multiple_of(q * CHUNK, CHUNK), CHUNK)], cbuf.at[slot], c_sem.at[slot])

    def out_copy(q):
        slot = lax.rem(q, 2)
        return pltpu.make_async_copy(
            obuf.at[slot], com.at[:, pl.ds(pl.multiple_of(q * CHUNK, CHUNK), CHUNK)], o_sem.at[slot])

    L, La = store_b.shape[0], store_a.shape[0]
    rows_b = pl.ds(na * S, L)
    rows_a = pl.ds(na * S + L, La)
    load_a = pltpu.make_async_copy(store_a, K.at[rows_a], l_sem.at[0])
    load_b = pltpu.make_async_copy(store_b, K.at[rows_b], l_sem.at[1])
    load_a.start()
    load_b.start()
    corr_copy(0).start()
    rs[...] = jnp.zeros_like(rs)

    def pick_a(h, dst):
        def body(i, carry):
            cols = pl.ds(pl.multiple_of(h * H + i * 128, 128), 128)
            dst[:, pl.ds(pl.multiple_of(i * 128, 128), 128)] = jnp.dot(
                hot_a[...], K[rows_a, cols], preferred_element_type=jnp.float32).astype(jnp.bfloat16)
            return carry

        lax.fori_loop(0, H // 128, body, 0)

    load_a.wait()
    pick_a(1 - c, asend)
    pl.semaphore_wait(barrier, na + nb - 2)

    part = pltpu.make_async_remote_copy(
        src_ref=asend, dst_ref=apart, send_sem=p_sem.at[0], recv_sem=p_sem.at[1],
        device_id=(ia, sib), device_id_type=MESH)
    part.start()

    def b_slot(s, t):
        return B.at[t, pl.ds(pl.multiple_of(s * S, 16), S)]

    def b_copy(up, s, t, source):
        return pltpu.make_async_remote_copy(
            src_ref=source, dst_ref=b_slot(s, t), send_sem=b_send.at[up, s, t], recv_sem=b_recv.at[s, t],
            device_id=(ia + 1 if up == 0 else ia - 1, ib), device_id_type=MESH)

    def b_own(t):
        cols = pl.ds(pl.multiple_of(t * CHUNK, CHUNK), CHUNK)
        B[t, pl.ds(pl.multiple_of(ia * S, 16), S), :] = jnp.dot(
            hot_b[...], K[rows_b, cols], preferred_element_type=jnp.float32).astype(jnp.bfloat16)

        @pl.when(ia < na - 1)
        def _():
            b_copy(0, ia, t, b_slot(ia, t)).start()

        @pl.when(ia > 0)
        def _():
            b_copy(1, ia, t, b_slot(ia, t)).start()

    last = 2 * (na - 1)

    def inside(i, d):
        return (i >= 2 * d) & (i < Q + 2 * d)

    def comm(i):
        @pl.when(inside(i, 0))
        def _():
            b_own(jnp.minimum(i, Q - 1))

        for d in range(1, na):
            u = jnp.clip(i - 2 * d, 0, Q - 1)

            def below(u=u, s=ia - d):
                b_copy(0, s, u, b_slot(s, u)).wait_recv()

                @pl.when(ia < na - 1)
                def _():
                    b_copy(0, s, u, b_slot(s, u)).start()

            def above(u=u, s=ia + d):
                b_copy(1, s, u, b_slot(s, u)).wait_recv()

                @pl.when(ia > 0)
                def _():
                    b_copy(1, s, u, b_slot(s, u)).start()

            pl.when(inside(i, d) & (ia - d >= 0))(below)
            pl.when(inside(i, d) & (ia + d < na))(above)

    def a_slot(p, h):
        return K.at[pl.ds(pl.multiple_of(p * S, 16), S), pl.ds(pl.multiple_of(h * H, 128), H)]

    def a_copy(p, d):
        return pltpu.make_async_remote_copy(
            src_ref=a_slot(p, c), dst_ref=a_slot(p, c), send_sem=a_send.at[d], recv_sem=a_recv.at[p, c],
            device_id=(ia, lax.rem(ib + 2 * d, nb)), device_id_type=MESH)

    def a_forward(p, h):
        return pltpu.make_async_remote_copy(
            src_ref=a_slot(p, h), dst_ref=a_slot(p, h), send_sem=f_send.at[p], recv_sem=a_recv.at[p, h],
            device_id=(ia, sib), device_id_type=MESH)

    load_b.wait()

    def early(t, carry):
        comm(t)
        return carry

    lax.fori_loop(0, 2, early, 0)
    part.wait()

    def merge(i, carry):
        here = pl.ds(pl.multiple_of(i * 128, 128), 128)
        cols = pl.ds(pl.multiple_of(c * H + i * 128, 128), 128)
        own = jnp.dot(hot_a[...], K[rows_a, cols], preferred_element_type=jnp.float32)
        K[pl.ds(pl.multiple_of(sa * S, 16), S), cols] = own.astype(jnp.bfloat16) + apart[:, here]
        return carry

    lax.fori_loop(0, H // 128, merge, 0)
    for d in range(1, na):
        a_copy(sa, d).start()
    a_forward(sa, c).start()

    lax.fori_loop(2, last + FIRST, early, 0)
    for d in range(1, na):
        p = lax.rem(sa + na - d, na)
        a_copy(p, d).wait_recv()
        a_forward(p, c).start()
    for p in range(na):
        a_forward(p, 1 - c).wait_recv()

    def turn(i, carry):
        cols = pl.ds(pl.multiple_of(i * 256, 256), 256)
        AT[cols, :] = K[0:na * S, cols].T
        return carry

    lax.fori_loop(0, W // 256, turn, 0)
    for d in range(1, na):
        a_copy(sa, d).wait_send()
    for p in range(na):
        a_forward(p, c).wait_send()

    ones = jnp.ones((16, CHUNK), jnp.bfloat16)

    def compute(q, carry):
        slot = lax.rem(q, 2)
        corr_copy(q).wait()

        @pl.when(q + 1 < Q)
        def _():
            corr_copy(q + 1).start()

        @pl.when(q >= 2)
        def _():
            out_copy(q - 2).wait()

        cols = pl.ds(pl.multiple_of(q * CHUNK, CHUNK), CHUNK)

        def block(r, carry):
            rows = pl.ds(pl.multiple_of(r * R, R), R)
            acc = jnp.dot(AT[rows, :], B[q], preferred_element_type=jnp.float32)
            cm = (decay_factor * cbuf[slot, rows, :].astype(jnp.float32)
                  + (1.0 - decay_factor) / GROUP * acc).astype(jnp.bfloat16)
            obuf[slot, rows, :] = cm
            e = jnp.exp(cm.astype(jnp.float32) * (1.0 / regularizer_strength)).astype(jnp.bfloat16)
            K[rows, cols] = e
            rs[:, rows] += lax.dot_general(
                ones, e, (((1,), (1,)), ((), ())), preferred_element_type=jnp.float32)
            return carry

        lax.fori_loop(0, W // R, block, 0)
        out_copy(q).start()
        return carry

    def done(t):
        return jnp.minimum(2 * (t - FIRST + 1), t + 1)

    def main(t, carry):
        comm(t + last)
        lax.fori_loop(done(t - 1), done(t), compute, 0)
        return carry

    lax.fori_loop(FIRST, Q, main, 0)

    def exchange(it, n, me, peer, buf, send, recv, partial):
        buf[it * n + me] = partial

        def copy(owner, d):
            return pltpu.make_async_remote_copy(
                src_ref=buf.at[it * n + owner], dst_ref=buf.at[it * n + owner],
                send_sem=send.at[it, d], recv_sem=recv.at[it, owner],
                device_id=peer(lax.rem(me + d, n)), device_id_type=MESH)

        for d in range(1, n):
            copy(me, d).start()
        for d in range(1, n):
            copy(lax.rem(me + n - d, n), d).wait_recv()
        total = buf[it * n]
        for j in range(1, n):
            total = total + buf[it * n + j]
        for d in range(1, n):
            copy(me, d).wait_send()
        return total

    def row_pass(colm):
        lhs = jnp.broadcast_to(colm, (16, W)).astype(jnp.bfloat16)

        def body(r, carry):
            rows = pl.ds(pl.multiple_of(r * R, R), R)
            rs[:, rows] = lax.dot_general(
                lhs, K[rows, :], (((1,), (1,)), ((), ())), preferred_element_type=jnp.float32)
            return carry

        lax.fori_loop(0, W // R, body, 0)
        return rs[0:1, :]

    def col_pass(srcm):
        lhs = jnp.broadcast_to(srcm, (16, W)).astype(jnp.bfloat16)

        def body(r, carry):
            cols = pl.ds(pl.multiple_of(r * R, R), R)
            rs[:, cols] = jnp.dot(lhs, K[:, cols], preferred_element_type=jnp.float32)
            return carry

        lax.fori_loop(0, W // R, body, 0)
        return rs[0:1, :]

    partial = rs[0:1, :]
    for it in range(ITERS):
        if it > 0:
            partial = row_pass(col_out[...])
        row = exchange(it, nb, ib, lambda j: (ia, j), rowx, r_send, r_recv, partial)
        src_out[...] = (nb * W) / row
        partial = col_pass(src_out[...])
        col = exchange(it, na, ia, lambda j: (j, ib), colx, k_send, k_recv, partial)
        col_out[...] = (na * W) / col

    for q in range(max(Q - 2, 0), Q):
        out_copy(q).wait()

    def drain(t, carry):
        for s in range(na):
            @pl.when((ia < na - 1) & (s <= ia))
            def _():
                b_copy(0, s, t, b_slot(s, t)).wait_send()

            @pl.when((ia > 0) & (s >= ia))
            def _():
                b_copy(1, s, t, b_slot(s, t)).wait_send()
        return carry

    lax.fori_loop(0, Q, drain, 0)


def fused(na, nb, S, W, hot_b, hot_a, store_b, store_a, corr):
    Q = W // CHUNK
    dma = pltpu.SemaphoreType.DMA
    any_space = pl.BlockSpec(memory_space=pl.ANY)
    vmem = pl.BlockSpec(memory_space=pltpu.VMEM)
    return pl.pallas_call(
        functools.partial(kernel, na, nb, S, W),
        out_shape=(
            jax.ShapeDtypeStruct((W, W), jnp.bfloat16),
            jax.ShapeDtypeStruct((1, W), jnp.float32),
            jax.ShapeDtypeStruct((1, W), jnp.float32),
        ),
        in_specs=[vmem] * 2 + [any_space] * 3,
        out_specs=(any_space, vmem, vmem),
        scratch_shapes=[
            pltpu.VMEM((W, W), jnp.bfloat16),
            pltpu.VMEM((W, na * S), jnp.bfloat16),
            pltpu.VMEM((Q, na * S, CHUNK), jnp.bfloat16),
            pltpu.VMEM((2, W, CHUNK), jnp.bfloat16),
            pltpu.VMEM((2, W, CHUNK), jnp.bfloat16),
            pltpu.VMEM((S, W // 2), jnp.bfloat16),
            pltpu.VMEM((S, W // 2), jnp.bfloat16),
            pltpu.VMEM((16, W), jnp.float32),
            pltpu.VMEM((ITERS * nb, 1, W), jnp.float32),
            pltpu.VMEM((ITERS * na, 1, W), jnp.float32),
            dma((2, na, Q)), dma((na, Q)),
            dma((na,)), dma((na, 2)), dma((na,)), dma((2,)), dma((2,)),
            dma((2,)), dma((2,)),
            dma((ITERS, nb)), dma((ITERS, nb)), dma((ITERS, na)), dma((ITERS, na)),
        ],
        compiler_params=pltpu.CompilerParams(
            collective_id=0, has_side_effects=True, vmem_limit_bytes=60 * 2**20),
        cost_estimate=pl.CostEstimate(
            flops=2 * GROUP * W * W, bytes_accessed=4 * W * W, transcendentals=W * W),
    )(hot_b, hot_a, store_b, store_a, corr)


def general(na, nb, corr_old, store_a, store_b, shuffle_order):
    rows_local = store_a.shape[0]
    chosen = jnp.zeros((shuffle_order.shape[0],), jnp.float32).at[shuffle_order[:GROUP]].set(1.0)
    kept_rows = lax.dynamic_slice_in_dim(chosen, lax.axis_index("ba") * rows_local, rows_local, 0)
    masked_a = store_a * kept_rows[:, None].astype(jnp.bfloat16)
    whole_a = lax.all_gather(masked_a, "ba", axis=0, tiled=True)
    summed = contract(whole_a, lax.all_gather(store_b, "aa", axis=0, tiled=True))
    com = (
        decay_factor * corr_old.astype(jnp.float32) + (1.0 - decay_factor) / GROUP * summed
    ).astype(jnp.bfloat16)
    K = jnp.exp(com.astype(jnp.float32) / regularizer_strength).astype(jnp.bfloat16)
    W = store_b.shape[1]
    col = jnp.ones((W,), jnp.float32)
    src = jnp.ones((store_a.shape[1],), jnp.float32)
    for _ in range(ITERS):
        src = nb * W / lax.psum(
            jnp.dot(K, col.astype(jnp.bfloat16), preferred_element_type=jnp.float32), "ba")
        col = na * store_a.shape[1] / lax.psum(
            jnp.dot(src.astype(jnp.bfloat16), K, preferred_element_type=jnp.float32), "aa")
    return com, src[None], col[None]


def shards(na, nb, corr_old, store_a, store_b, shuffle_order):
    ia, ib = lax.axis_index("aa"), lax.axis_index("ba")
    L, La = store_b.shape[0], store_a.shape[0]
    W = store_b.shape[1]
    step = max(16, 128 // na)
    S = -(-(GROUP // na + 32) // step) * step
    group = shuffle_order[:GROUP]
    owner = group // L
    order = jnp.arange(GROUP)

    def slots(seg):
        mine = owner == seg
        rank = jnp.sum((mine[None, :] & (order[None, :] < order[:, None])).astype(jnp.int32), axis=1)
        hit = mine[None, :] & (rank[None, :] == jnp.arange(S)[:, None])
        return jnp.sum(jnp.where(hit, group[None, :] + 1, 0), axis=1) - 1

    def hot(rows, first, n):
        return (rows[:, None] == first + jnp.arange(n)[None, :]).astype(jnp.bfloat16)

    fits = jnp.max(jnp.sum((owner[:, None] == jnp.arange(na)[None, :]).astype(jnp.int32), axis=0)) <= S

    def fast(corr_old, store_a, store_b, shuffle_order):
        return fused(
            na, nb, S, W, hot(slots(ia), ia * L, L), hot(slots(ib // 2), ib * La, La),
            store_b, store_a, corr_old)
    com, src, col = lax.cond(
        fits, fast, functools.partial(general, na, nb), corr_old, store_a, store_b, shuffle_order)
    return com, src[0], col[0]


def solution(mesh):
    na, nb = mesh.shape["aa"], mesh.shape["ba"]
    in_specs = (P("aa", "ba"), P("ba", "aa"), P("aa", "ba"), P())
    out_specs = (P("aa", "ba"), P("aa"), P("ba"))
    return jax.shard_map(
        functools.partial(shards, na, nb), mesh=mesh, in_specs=in_specs, out_specs=out_specs, check_vma=False)
```
